32 devices in a mesh: groups: 2 (over x), fsdp: 16 (over z, y, core).
Axes of the slice: x: 2, y: 2, z: 4, core: 2. Of those that a mesh axis runs over, the one named last changes fastest.
Arguments:
- inputs: bfloat16 [10240, 8192], P(('groups', 'fsdp')), parts along dimension 0, may hold values from -6 to 6
- key_value_gradient: bfloat16 [10240, 2048], P(('groups', 'fsdp')), parts along dimension 0, may hold values from -6 to 6
- kept_frozen_blocks: bfloat16 [2, 320, 128, 128], P(None, 'fsdp'), may hold values from -0.25 to 0.25
- kept: int32 [2, 64, 8], replicated, may hold values from 0 to 1, as said below
- adapter_down_matrices: bfloat16 [16384, 128], P(('groups', 'fsdp')), parts along dimension 0, may hold values from -0.1875 to 0.1875
- adapter_up_matrices: bfloat16 [4, 64, 1024], P('groups'), parts along dimension 0, may hold values from -0.1875 to 0.1875
Outputs:
- grad_inputs: bfloat16 [10240, 8192], P(('groups', 'fsdp')), parts along dimension 0
- grad_down: float32 [16384, 128], P(('groups', 'fsdp')), parts along dimension 0
- grad_up: float32 [4, 64, 1024], P('groups'), parts along dimension 0
The draws below stay inside these ranges and needn't reach their ends.
There are 2 independent parts, one for each index of `groups`. The reference program is written for one: setup_inputs(seed, part) draws one part's arguments, and reference() takes and returns one part's arrays. A program takes and returns all parts, laid end to end along the dimension named above; an argument that names none is the same for every part. Nothing has to cross between parts.
Inputs may be any that keep to these rules, and one draw needn't show every extreme that they name: `kept`: each block-row keeps 3 to 5 blocks; block-rows r and r + 32 of one projection keep 8 blocks together; the block-rows s * 4 to (s + 1) * 4 - 1 keep at most 20 blocks of a projection, and some such set keeps exactly 20.
All inputs are finite; a program needn't handle non-finite values.
Results may differ from the reference program's by a relative error of at most 0.003.
Values may be sent and summed in bfloat16 or wider, within the bound.
A program may use at most 128 MiB of HBM per device.

```python
import math
import jax
import jax.numpy as jnp
from jax import lax

MODEL_WIDTH = 8192
KEY_VALUE_WIDTH = 1024
ADAPTER_RANK = 64
BLK = 128
TOKEN_COUNT = 5120
NB = 64
KB = 8
SLOTS = 20
N_FSDP = 16


def draw_kept(key, part):
    key = jax.random.fold_in(key, 7)
    row_blocks = MODEL_WIDTH // BLK
    col_blocks = KEY_VALUE_WIDTH // BLK
    half_rows = row_blocks // 2
    per_shard = row_blocks // N_FSDP
    key_delta, key_shard, key_order = jax.random.split(key, 3)
    row_delta = jax.random.randint(key_delta, (2, half_rows), -1, 2)
    chosen = jax.random.randint(key_shard, (2, 1), 0, N_FSDP)
    row_index = jnp.arange(half_rows, dtype=jnp.int32)[None, :]
    inside = row_index // per_shard == chosen % (N_FSDP // 2)
    forced = jnp.where(chosen < N_FSDP // 2, 1, -1)
    row_delta = jnp.where(inside, forced, row_delta)
    counts = jnp.concatenate([col_blocks // 2 + row_delta, col_blocks // 2 - row_delta], axis=1)
    ranking = jax.vmap(lambda subkey: jax.random.permutation(subkey, col_blocks))(jax.random.split(key_order, 2 * row_blocks))
    ranking = ranking.reshape(2, row_blocks, col_blocks)
    return (ranking < counts[:, :, None]).astype(jnp.int32)


def with_spikes(result, rng, source, target, parts, factor):
    def block_of(dim):
        return (jnp.arange(result.shape[dim]) // (result.shape[dim] // parts)).reshape((-1,) + (1,) * (result.ndim - 1 - dim))

    one_side = jax.random.permutation(rng, parts)[block_of(target)]
    second = (block_of(target) + parts // 2) % parts
    return jnp.where((block_of(source) == one_side) | (block_of(source) == second), factor * result, result)


def level_of(stream_key, extent, cuts, smallest, top_value):
    def one(dim, shards_of):
        steps = jax.random.uniform(jax.random.fold_in(jax.random.fold_in(stream_key, 6), dim), (shards_of,), jnp.float32, smallest / len(cuts), top_value / len(cuts))
        return jnp.repeat(jnp.exp(steps), extent[dim] // shards_of).reshape((-1,) + (1,) * (len(extent) - dim - 1))

    gain = one(*cuts[0])
    for cut in cuts[1:]:
        gain = gain * one(*cut)
    return gain


def normal_values(stream_key, dims, spread, most, cuts=(), kind=jnp.bfloat16):
    array = jax.random.normal(stream_key, dims, jnp.float32) * spread
    if len(cuts) > 0:
        array = level_of(stream_key, dims, cuts, -0.22, 0.18) * array
    return jnp.clip(array, min=-most, max=most).astype(kind)


def noise_with(rng, extent, spread, limit, pieces, heavy, held_as=jnp.bfloat16):
    array = spread * jax.random.normal(rng, extent, jnp.float32)
    if pieces:
        array = array * level_of(rng, extent, pieces, -0.22, 0.18)
    return jnp.clip(with_spikes(array, jax.random.fold_in(rng, 3), *heavy), -limit, limit).astype(held_as)


def setup_inputs(seed: int = 0, part: int = 0) -> dict:
    arg_keys = jax.random.split(jax.random.key(seed), 7)
    own_keys = jax.random.split(jax.random.fold_in(arg_keys[6], part), 7)
    inputs = noise_with(own_keys[0], (TOKEN_COUNT, MODEL_WIDTH), 1.0, 6.0, ((0, 16),), (0, 1, 16, 2.0))
    key_value_gradient = normal_values(own_keys[1], (TOKEN_COUNT, 2 * KEY_VALUE_WIDTH), 1.0, 6.0, ((0, 16),))
    kept_frozen_blocks = normal_values(arg_keys[2], (2, NB * (KB // 2 + 1), BLK, BLK), (KEY_VALUE_WIDTH // 2) ** -0.5, 0.25, ((1, 16),))
    kept = draw_kept(jax.random.fold_in(arg_keys[6], 71), part)
    adapter_down_matrices = normal_values(own_keys[4], (MODEL_WIDTH, 2 * ADAPTER_RANK), (ADAPTER_RANK * 16) ** -0.5, 0.1875, ((0, 16),))
    adapter_up_matrices = normal_values(own_keys[5], (2, ADAPTER_RANK, KEY_VALUE_WIDTH), KEY_VALUE_WIDTH ** -0.5, 0.1875)
    return {"inputs": inputs, "key_value_gradient": key_value_gradient, "kept_frozen_blocks": kept_frozen_blocks, "kept": kept, "adapter_down_matrices": adapter_down_matrices, "adapter_up_matrices": adapter_up_matrices}


adapter_scale = 0.5

def dense_weights(kept_frozen_blocks, kept):
    row_blocks = MODEL_WIDTH // BLK
    col_blocks = KEY_VALUE_WIDTH // BLK
    per_shard = row_blocks // N_FSDP
    flat_kept = kept.reshape(2, N_FSDP, per_shard * col_blocks)
    before = (jnp.cumsum(flat_kept, axis=-1) - flat_kept).reshape(2, row_blocks, col_blocks)
    shard_of = (jnp.arange(row_blocks, dtype=jnp.int32) // per_shard)[None, :, None]
    slot_table = jnp.where(kept > 0, shard_of * SLOTS + before, 0).astype(jnp.int32)
    taken = jax.vmap(lambda blocks, indices: jnp.take(blocks, indices.reshape(-1), axis=0))(kept_frozen_blocks, slot_table)
    taken = taken.reshape(2, row_blocks, col_blocks, BLK, BLK)
    dense_blocks = jnp.where(kept[..., None, None] > 0, taken, jnp.zeros((), kept_frozen_blocks.dtype))
    return dense_blocks.transpose(0, 1, 3, 2, 4).reshape(2, MODEL_WIDTH, KEY_VALUE_WIDTH)

def token_sum(left_side, right_side):
    return lax.dot_general(left_side, right_side, (((0,), (0,)), ((), ())), preferred_element_type=jnp.float32)

def reference(inputs, key_value_gradient, kept_frozen_blocks, kept, adapter_down_matrices, adapter_up_matrices):
    weights = dense_weights(kept_frozen_blocks, kept)
    key_gradient = key_value_gradient[:, :KEY_VALUE_WIDTH]
    value_gradient = key_value_gradient[:, KEY_VALUE_WIDTH:]
    low_rank_product = jnp.concatenate([jnp.dot(key_gradient, adapter_up_matrices[0].T, preferred_element_type=jnp.float32), jnp.dot(value_gradient, adapter_up_matrices[1].T, preferred_element_type=jnp.float32)], axis=1).astype(jnp.bfloat16)
    hidden_states = jnp.dot(inputs, adapter_down_matrices, preferred_element_type=jnp.float32).astype(jnp.bfloat16)
    gradient_total = jnp.dot(key_gradient, weights[0].T, preferred_element_type=jnp.float32)
    gradient_total = gradient_total + jnp.dot(value_gradient, weights[1].T, preferred_element_type=jnp.float32)
    gradient_total = gradient_total + adapter_scale * jnp.dot(low_rank_product, adapter_down_matrices.T, preferred_element_type=jnp.float32)
    grad_inputs = gradient_total.astype(jnp.bfloat16)
    gradient_scale = adapter_scale / math.sqrt(TOKEN_COUNT)
    grad_down = gradient_scale * token_sum(inputs, low_rank_product)
    grad_up = gradient_scale * jnp.stack([token_sum(hidden_states[:, :ADAPTER_RANK], key_gradient), token_sum(hidden_states[:, ADAPTER_RANK:], value_gradient)])
    return (grad_inputs, grad_down, grad_up)
```

```python
import functools
import math

import jax
import jax.numpy as jnp
from jax import lax
from jax.experimental import pallas as pl
from jax.experimental.pallas import tpu as pltpu
from jax.sharding import PartitionSpec as P

adapter_scale = 0.5
F32 = jnp.float32
BF16 = jnp.bfloat16


def dot(a, b, ca, cb):
    return lax.dot_general(a, b, (((ca,), (cb,)), ((), ())), preferred_element_type=F32)


def exchange_kernel(
    n,
    scale,
    count_ref,
    x_ref,
    g_ref,
    kfb_ref,
    a_ref,
    b_ref,
    wbuf,
    abuf,
    low_ref,
    down_ref,
    ubuf,
    wown,
    ovf,
    parts,
    rc,
    ry,
    rz,
    uparts,
    uc,
    uy,
    uz,
    asem,
    wsem_z,
    wsem_y,
    wsem_x,
    wsem_c,
    osem,
    dsem,
    dzsem,
    usem,
    uzsem,
    gsem,
    lsem,
):
    zs = n // 4
    group = lax.axis_index("groups")
    me = lax.axis_index("fsdp")
    k = lax.rem(me, 2)
    y = lax.rem(me // 2, 2)
    z = me // 4
    m = lax.rem(group, 2)
    other_group = group + 1 - 2 * m

    def place(dz, dy, dk):
        zz = lax.rem(z + dz, zs)
        yy = y if dy == 0 else 1 - y
        kk = k if dk == 0 else 1 - k
        return (zz * 2 + yy) * 2 + kk

    def device(dz=0, dy=0, dk=0, dx=0):
        return (group if dx == 0 else other_group, place(dz % zs, dy, dk))

    sends = []

    def send(src, dst, ssem, rsem, target):
        copy = pltpu.make_async_remote_copy(
            src_ref=src,
            dst_ref=dst,
            send_sem=ssem,
            recv_sem=rsem,
            device_id=target,
            device_id_type=pl.DeviceIdType.MESH,
        )
        copy.start()
        sends.append(copy)

    def arrived(ref, ssem, rsem, source):
        pltpu.make_async_remote_copy(
            src_ref=ref,
            dst_ref=ref,
            send_sem=ssem,
            recv_sem=rsem,
            device_id=source,
            device_id_type=pl.DeviceIdType.MESH,
        ).wait_recv()

    sibling = device(dk=1)
    across_y = device(dy=1)
    across_x = device(dx=1)
    partners = [sibling, across_y, across_x] + [device(dz=dz) for dz in range(1, zs)]
    barrier = pltpu.get_barrier_semaphore()
    for partner in partners:
        pl.semaphore_signal(
            barrier, inc=1, device_id=partner, device_id_type=pl.DeviceIdType.MESH
        )
    pl.semaphore_wait(barrier, len(partners))

    def gather_start(buf, sem):
        own = buf.at[me]
        for dz in range(1, zs):
            send(own, own, sem.at[0, 0, dz], sem.at[0, 1, dz], device(dz=-dz))
        send(own, own, sem.at[1, 0, 0], sem.at[1, 1, 0], across_y)
        send(own, own, sem.at[2, 0, 0], sem.at[2, 1, 0], sibling)

    def gather_middle(buf, sem):
        for dz in range(1, zs):
            piece = buf.at[place(dz, 0, 0)]
            arrived(piece, sem.at[0, 0, dz], sem.at[0, 1, dz], device(dz=dz))
            send(piece, piece, sem.at[1, 0, dz], sem.at[1, 1, dz], across_y)
            send(piece, piece, sem.at[2, 0, dz], sem.at[2, 1, dz], sibling)
        for dz in range(zs):
            piece = buf.at[place(dz, 1, 0)]
            arrived(piece, sem.at[1, 0, dz], sem.at[1, 1, dz], across_y)
            send(piece, piece, sem.at[2, 0, zs + dz], sem.at[2, 1, zs + dz], sibling)

    def gather_end(buf, sem):
        for dz in range(zs):
            for dy in range(2):
                slot = dy * zs + dz
                arrived(
                    buf.at[place(dz, dy, 1)], sem.at[2, 0, slot], sem.at[2, 1, slot], sibling
                )

    slots = kfb_ref.shape[1]
    per_shard = slots // 5
    full = 4 * per_shard
    least = 3 * per_shard

    send(kfb_ref.at[:, pl.ds(full, per_shard)], ovf, osem.at[0], osem.at[1], device(dz=zs // 2))
    abuf[me] = a_ref[...]
    gather_start(abuf, asem)

    wown[:, 0:least] = kfb_ref[:, 0:least]
    rank = b_ref.shape[1]
    width = b_ref.shape[2]
    lows = [dot(g_ref[:, p * width : (p + 1) * width], b_ref[p], 1, 1) for p in range(2)]
    low_ref[...] = jnp.concatenate(lows, axis=1).astype(BF16)

    arrived(ovf, osem.at[0], osem.at[1], device(dz=zs // 2))
    for p in range(2):
        held = count_ref[p]
        for t in range(per_shard):
            slot = least + t
            extra = ovf[p, jnp.clip(slot - held, 0, per_shard - 1)]
            wown[p, slot] = jnp.where(slot < held, kfb_ref[p, slot], extra)

    mine = wown.at[m]
    for dz in range(1, zs):
        send(mine, wbuf.at[m, me], wsem_z.at[0, dz], wsem_z.at[1, dz], device(dz=-dz))
    send(mine, wbuf.at[m, me], wsem_y.at[0, 0], wsem_y.at[1, 0], across_y)
    send(mine, wbuf.at[m, me], wsem_c.at[0, 0, 0], wsem_c.at[1, 0, 0], sibling)
    send(wown.at[1 - m], wbuf.at[1 - m, me], wsem_c.at[0, 1, 0], wsem_c.at[1, 1, 0], sibling)
    keep_own = pltpu.make_async_copy(wown, wbuf.at[:, me], lsem)
    keep_own.start()

    low_t = low_ref[...].astype(F32).T.astype(BF16)
    cols = a_ref.shape[0]

    def down_parts(dk):
        kk = k if dk == 0 else 1 - k
        for yy in range(2):

            def body(zz, carry):
                owner = (zz * 2 + yy) * 2 + kk
                at = pl.ds(pl.multiple_of(owner * cols, cols), cols)
                parts[dk, yy, zz] = scale * dot(low_t, x_ref[:, at], 1, 0)
                return carry

            lax.fori_loop(0, zs, body, 0)

    down_parts(1)
    send(parts.at[1], rc, dsem.at[0, 0], dsem.at[0, 1], sibling)
    down_parts(0)

    def w_from_z(dz):
        piece = wbuf.at[m, place(dz, 0, 0)]
        arrived(piece, wsem_z.at[0, dz], wsem_z.at[1, dz], device(dz=dz))
        send(piece, piece, wsem_y.at[0, dz], wsem_y.at[1, dz], across_y)
        send(piece, piece, wsem_x.at[0, dz], wsem_x.at[1, dz], across_x)
        send(piece, piece, wsem_c.at[0, 0, dz], wsem_c.at[1, 0, dz], sibling)

    def w_from_y(dz):
        slot = zs + dz
        piece = wbuf.at[m, place(dz, 1, 0)]
        arrived(piece, wsem_y.at[0, dz], wsem_y.at[1, dz], across_y)
        send(piece, piece, wsem_x.at[0, slot], wsem_x.at[1, slot], across_x)
        send(piece, piece, wsem_c.at[0, 0, slot], wsem_c.at[1, 0, slot], sibling)

    def w_from_x(dz, dy):
        slot = dy * zs + dz
        piece = wbuf.at[1 - m, place(dz, dy, 0)]
        arrived(piece, wsem_x.at[0, slot], wsem_x.at[1, slot], across_x)
        send(piece, piece, wsem_c.at[0, 1, slot], wsem_c.at[1, 1, slot], sibling)

    def reduce_y(own, received, landing, ssem, rsem):
        own[0, 1 - y] = own[0, 1 - y] + received[1 - y]
        send(own.at[0, 1 - y], landing, ssem, rsem, across_y)
        own[0, y] = own[0, y] + received[y]

    def reduce_z(own, received, landing, sem):
        own[0, y] = own[0, y] + received[...]
        for dz in range(1, zs):
            send(
                own.at[0, y, lax.rem(z + zs - dz, zs)],
                landing.at[dz],
                sem.at[0, dz],
                sem.at[1, dz],
                device(dz=-dz),
            )

    def reduce_end(own, landing, sem):
        total = own[0, y, z]
        for dz in range(1, zs):
            arrived(landing.at[dz], sem.at[0, dz], sem.at[1, dz], device(dz=dz))
            total = total + landing[dz]
        return total

    gather_middle(abuf, asem)
    arrived(rc, dsem.at[0, 0], dsem.at[0, 1], sibling)
    reduce_y(parts, rc, ry, dsem.at[1, 0], dsem.at[1, 1])
    w_from_z(1)
    w_from_y(0)
    arrived(ry, dsem.at[1, 0], dsem.at[1, 1], across_y)
    reduce_z(parts, ry, rz, dzsem)
    gather_end(abuf, asem)

    hidden = jnp.zeros((x_ref.shape[0], 2 * rank), F32)

    def hidden_step(owner, total):
        at = pl.ds(pl.multiple_of(owner * cols, cols), cols)
        return total + dot(x_ref[:, at], abuf[owner], 1, 0)

    hidden = lax.fori_loop(0, n, hidden_step, hidden).astype(BF16)
    rows = 2 * rank // n
    hidden_t = hidden.astype(F32).T.astype(BF16)
    ups = scale * jnp.concatenate(
        [
            dot(hidden_t[p * rank : (p + 1) * rank], g_ref[:, p * width : (p + 1) * width], 1, 0)
            for p in range(2)
        ],
        axis=0,
    )
    for owner in range(n):
        kk, yy, zz = owner % 2, owner // 2 % 2, owner // 4
        dk = lax.rem(k + kk, 2)
        uparts[dk, yy, zz] = ups[owner * rows : (owner + 1) * rows]
    send(uparts.at[1], uc, usem.at[0, 0], usem.at[0, 1], sibling)

    for dz in range(2, zs):
        w_from_z(dz)
        w_from_y(dz - 1)
        if dz == 2:
            arrived(uc, usem.at[0, 0], usem.at[0, 1], sibling)
            reduce_y(uparts, uc, uy, usem.at[1, 0], usem.at[1, 1])
    arrived(uy, usem.at[1, 0], usem.at[1, 1], across_y)
    reduce_z(uparts, uy, uz, uzsem)
    w_from_x(1, 0)
    w_from_x(0, 1)
    down_ref[...] = reduce_end(parts, rz, dzsem)
    w_from_y(zs - 1)
    ubuf[me] = reduce_end(uparts, uz, uzsem)
    gather_start(ubuf, gsem)
    for dz in range(2, zs):
        w_from_x(dz, 0)
        w_from_x(dz - 1, 1)
        if dz == 2:
            gather_middle(ubuf, gsem)
    w_from_x(zs - 1, 1)
    gather_end(ubuf, gsem)
    for p in range(2):
        at = m if p == 0 else 1 - m
        for dz in range(zs):
            for dy in range(2):
                slot = dy * zs + dz
                arrived(
                    wbuf.at[at, place(dz, dy, 1)],
                    wsem_c.at[0, p, slot],
                    wsem_c.at[1, p, slot],
                    sibling,
                )
    for copy in sends:
        copy.wait_send()
    keep_own.wait()


def rows_kernel(row_blocks, table_ref, w_ref, a_ref, g_ref, low_ref, out_ref, dense):
    shard = pl.program_id(1) * pl.num_programs(0) + pl.program_id(0)
    full = w_ref.shape[3]
    block = w_ref.shape[-1]
    per_shard = out_ref.shape[1] // block
    col_blocks = g_ref.shape[1] // (2 * block)
    zero = jnp.zeros((block, block), BF16)
    for m in range(2):
        for r in range(per_shard):
            for c in range(col_blocks):
                code = table_ref[(m * row_blocks + shard * per_shard + r) * col_blocks + c]
                at = jnp.maximum(code, 0)
                taken = w_ref[m, at // full, 0, lax.rem(at, full)]
                col = (m * col_blocks + c) * block
                dense[r * block : (r + 1) * block, col : col + block] = jnp.where(
                    code >= 0, taken, zero
                )
    total = dot(g_ref[...], dense[...], 1, 1)
    total = total + adapter_scale * dot(low_ref[...], a_ref[...], 1, 1)
    out_ref[...] = total.astype(BF16)


def on_device(
    inputs, key_value_gradient, kept_frozen_blocks, kept, adapter_down_matrices, adapter_up_matrices
):
    n = lax.axis_size("fsdp")
    zs = n // 4
    tokens, model_width = inputs.shape
    slot_count = kept_frozen_blocks.shape[1]
    block = kept_frozen_blocks.shape[-1]
    row_blocks, col_blocks = kept.shape[1:]
    per_shard = row_blocks // n
    full = 4 * per_shard
    rank, width = adapter_up_matrices.shape[1:]
    cols = adapter_down_matrices.shape[0]
    rows = 2 * rank // n
    scale = adapter_scale / math.sqrt(tokens * n)

    flat = kept.reshape(2, n, per_shard * col_blocks)
    before = jnp.cumsum(flat, axis=-1) - flat
    counts = flat.sum(axis=-1)
    half = (jnp.arange(n, dtype=jnp.int32) // (n // 2))[None, :, None]
    code = jnp.where(
        before < full,
        half * full + before,
        (1 - half) * full + (2 * full - counts[:, :, None]) + before - full,
    )
    table = jnp.where(flat > 0, code, -1).reshape(-1).astype(jnp.int32)
    own_counts = lax.dynamic_index_in_dim(counts, lax.axis_index("fsdp"), 1, keepdims=False)

    vmem = pl.BlockSpec(memory_space=pltpu.VMEM)
    smem = pl.BlockSpec(memory_space=pltpu.SMEM)
    hbm = pl.BlockSpec(memory_space=pl.ANY)
    dma = pltpu.SemaphoreType.DMA
    wbuf, abuf, low, down_t, ubuf = pl.pallas_call(
        functools.partial(exchange_kernel, n, scale),
        out_shape=(
            jax.ShapeDtypeStruct((2, n, full, block, block), BF16),
            jax.ShapeDtypeStruct((n, cols, 2 * rank), BF16),
            jax.ShapeDtypeStruct((tokens, 2 * rank), BF16),
            jax.ShapeDtypeStruct((2 * rank, cols), F32),
            jax.ShapeDtypeStruct((n, rows, width), F32),
        ),
        in_specs=[smem, vmem, vmem, vmem, vmem, vmem],
        out_specs=(hbm, vmem, vmem, vmem, vmem),
        scratch_shapes=[
            pltpu.VMEM((2, full, block, block), BF16),
            pltpu.VMEM((2, per_shard, block, block), BF16),
            pltpu.VMEM((2, 2, zs, 2 * rank, cols), F32),
            pltpu.VMEM((2, zs, 2 * rank, cols), F32),
            pltpu.VMEM((zs, 2 * rank, cols), F32),
            pltpu.VMEM((zs, 2 * rank, cols), F32),
            pltpu.VMEM((2, 2, zs, rows, width), F32),
            pltpu.VMEM((2, zs, rows, width), F32),
            pltpu.VMEM((zs, rows, width), F32),
            pltpu.VMEM((zs, rows, width), F32),
            dma((3, 2, 2 * zs)),
            dma((2, zs)),
            dma((2, zs)),
            dma((2, 2 * zs)),
            dma((2, 2, 2 * zs)),
            dma((2,)),
            dma((2, 2)),
            dma((2, zs)),
            dma((2, 2)),
            dma((2, zs)),
            dma((3, 2, 2 * zs)),
            dma(()),
        ],
        compiler_params=pltpu.CompilerParams(
            collective_id=0, has_side_effects=True, vmem_limit_bytes=48 * 2**20
        ),
        name="exchange",
    )(
        own_counts,
        inputs,
        key_value_gradient,
        kept_frozen_blocks,
        adapter_down_matrices,
        adapter_up_matrices,
    )

    shard_cols = per_shard * block
    grad_inputs = pl.pallas_call(
        functools.partial(rows_kernel, row_blocks),
        out_shape=jax.ShapeDtypeStruct((tokens, model_width), BF16),
        grid_spec=pltpu.PrefetchScalarGridSpec(
            num_scalar_prefetch=1,
            grid=(n // 2, 2),
            in_specs=[
                pl.BlockSpec(
                    (2, 2, 1, full, block, block), lambda p, h, t: (0, 0, p, 0, 0, 0)
                ),
                pl.BlockSpec((shard_cols, 2 * rank), lambda p, h, t: (h * (n // 2) + p, 0)),
                pl.BlockSpec((tokens, 2 * width), lambda p, h, t: (0, 0)),
                pl.BlockSpec((tokens, 2 * rank), lambda p, h, t: (0, 0)),
            ],
            out_specs=pl.BlockSpec((tokens, shard_cols), lambda p, h, t: (0, h * (n // 2) + p)),
            scratch_shapes=[pltpu.VMEM((shard_cols, 2 * width), BF16)],
        ),
        compiler_params=pltpu.CompilerParams(vmem_limit_bytes=40 * 2**20),
        name="rows",
    )(
        table,
        wbuf.reshape(2, 2, n // 2, full, block, block),
        abuf.reshape(n * cols, 2 * rank),
        key_value_gradient,
        low,
    )
    return grad_inputs, down_t.T, ubuf.reshape(2, rank, width)


def solution(mesh):
    return jax.shard_map(
        on_device,
        mesh=mesh,
        in_specs=(
            P(("groups", "fsdp"), None),
            P(("groups", "fsdp"), None),
            P(None, "fsdp", None, None),
            P(),
            P(("groups", "fsdp"), None),
            P("groups", None, None),
        ),
        out_specs=(
            P(("groups", "fsdp"), None),
            P(("groups", "fsdp"), None),
            P("groups", None, None),
        ),
        check_vma=False,
    )
```

```python
import functools
import math

import jax
import jax.numpy as jnp
from jax import lax
from jax.experimental import pallas as pl
from jax.experimental.pallas import tpu as pltpu
from jax.sharding import PartitionSpec as P

adapter_scale = 0.5
F32 = jnp.float32
BF16 = jnp.bfloat16


def dot(a, b, ca, cb):
    return lax.dot_general(a, b, (((ca,), (cb,)), ((), ())), preferred_element_type=F32)


def exchange_kernel(
    n,
    scale,
    count_ref,
    x_ref,
    g_ref,
    kfb_ref,
    a_ref,
    b_ref,
    wbuf,
    abuf,
    low_ref,
    down_ref,
    ubuf,
    wown,
    ovf,
    parts,
    rc,
    ry,
    rz,
    uparts,
    uc,
    uy,
    uz,
    asem,
    wsem_z,
    wsem_y,
    wsem_x,
    wsem_c,
    osem,
    dsem,
    dzsem,
    usem,
    uzsem,
    gsem,
    lsem,
):
    zs = n // 4
    group = lax.axis_index("groups")
    me = lax.axis_index("fsdp")
    k = lax.rem(me, 2)
    y = lax.rem(me // 2, 2)
    z = me // 4
    m = lax.rem(group, 2)
    other_group = group + 1 - 2 * m

    def place(dz, dy, dk):
        zz = lax.rem(z + dz, zs)
        yy = y if dy == 0 else 1 - y
        kk = k if dk == 0 else 1 - k
        return (zz * 2 + yy) * 2 + kk

    def device(dz=0, dy=0, dk=0, dx=0):
        return (group if dx == 0 else other_group, place(dz % zs, dy, dk))

    sends = []

    def send(src, dst, ssem, rsem, target, when=None):
        copy = pltpu.make_async_remote_copy(
            src_ref=src,
            dst_ref=dst,
            send_sem=ssem,
            recv_sem=rsem,
            device_id=target,
            device_id_type=pl.DeviceIdType.MESH,
        )
        if when is None:
            copy.start()
        else:
            pl.when(when)(copy.start)
        sends.append((copy, when))

    def arrived(ref, ssem, rsem, source):
        pltpu.make_async_remote_copy(
            src_ref=ref,
            dst_ref=ref,
            send_sem=ssem,
            recv_sem=rsem,
            device_id=source,
            device_id_type=pl.DeviceIdType.MESH,
        ).wait_recv()

    sibling = device(dk=1)
    across_y = device(dy=1)
    across_x = device(dx=1)
    partners = [sibling, across_y, across_x] + [device(dz=dz) for dz in range(1, zs)]
    barrier = pltpu.get_barrier_semaphore()
    for partner in partners:
        pl.semaphore_signal(
            barrier, inc=1, device_id=partner, device_id_type=pl.DeviceIdType.MESH
        )
    pl.semaphore_wait(barrier, len(partners))

    def gather_start(buf, sem):
        own = buf.at[me]
        for dz in range(1, zs):
            send(own, own, sem.at[0, 0, dz], sem.at[0, 1, dz], device(dz=-dz))
        send(own, own, sem.at[1, 0, 0], sem.at[1, 1, 0], across_y)
        send(own, own, sem.at[2, 0, 0], sem.at[2, 1, 0], sibling)

    def gather_middle(buf, sem):
        for dz in range(1, zs):
            piece = buf.at[place(dz, 0, 0)]
            arrived(piece, sem.at[0, 0, dz], sem.at[0, 1, dz], device(dz=dz))
            send(piece, piece, sem.at[1, 0, dz], sem.at[1, 1, dz], across_y)
            send(piece, piece, sem.at[2, 0, dz], sem.at[2, 1, dz], sibling)
        for dz in range(zs):
            piece = buf.at[place(dz, 1, 0)]
            arrived(piece, sem.at[1, 0, dz], sem.at[1, 1, dz], across_y)
            send(piece, piece, sem.at[2, 0, zs + dz], sem.at[2, 1, zs + dz], sibling)

    def gather_end(buf, sem):
        for dz in range(zs):
            for dy in range(2):
                slot = dy * zs + dz
                arrived(
                    buf.at[place(dz, dy, 1)], sem.at[2, 0, slot], sem.at[2, 1, slot], sibling
                )

    slots = kfb_ref.shape[1]
    per_shard = slots // 5
    full = 4 * per_shard
    least = 3 * per_shard

    send(kfb_ref.at[:, pl.ds(full, per_shard)], ovf, osem.at[0], osem.at[1], device(dz=zs // 2))
    abuf[me] = a_ref[...]
    gather_start(abuf, asem)

    half = full // 2

    def chunk(p, owner, c):
        return wbuf.at[p, owner, pl.ds(c * half, half)]

    def w_start(own, c):
        mine = own.at[m, pl.ds(0, half)]
        to = chunk(m, me, c)
        send(
            mine,
            to,
            wsem_z.at[0, c, 0, 1],
            wsem_z.at[1, c, 0, 1],
            device(dz=-1),
            z > 0,
        )
        send(
            mine,
            to,
            wsem_z.at[0, c, 0, zs - 1],
            wsem_z.at[1, c, 0, zs - 1],
            device(dz=1),
            z < zs - 1,
        )
        send(mine, to, wsem_y.at[0, c, 0], wsem_y.at[1, c, 0], across_y)
        for p in range(2):
            at = m if p == 0 else 1 - m
            send(
                own.at[at, pl.ds(0, half)],
                chunk(at, me, c),
                wsem_c.at[0, p, c, 0],
                wsem_c.at[1, p, c, 0],
                sibling,
            )

    w_start(kfb_ref, 0)
    keep_first = pltpu.make_async_copy(
        kfb_ref.at[:, pl.ds(0, half)], wbuf.at[:, me, pl.ds(0, half)], lsem.at[0]
    )
    keep_first.start()

    wown[:, 0 : least - half] = kfb_ref[:, half:least]
    rank = b_ref.shape[1]
    width = b_ref.shape[2]
    lows = [dot(g_ref[:, p * width : (p + 1) * width], b_ref[p], 1, 1) for p in range(2)]
    low_ref[...] = jnp.concatenate(lows, axis=1).astype(BF16)

    arrived(ovf, osem.at[0], osem.at[1], device(dz=zs // 2))
    for p in range(2):
        held = count_ref[p]
        for t in range(per_shard):
            slot = least + t
            extra = ovf[p, jnp.clip(slot - held, 0, per_shard - 1)]
            wown[p, slot - half] = jnp.where(slot < held, kfb_ref[p, slot], extra)

    w_start(wown, 1)
    keep_second = pltpu.make_async_copy(
        wown, wbuf.at[:, me, pl.ds(half, half)], lsem.at[1]
    )
    keep_second.start()

    low_t = low_ref[...].astype(F32).T.astype(BF16)
    cols = a_ref.shape[0]

    def down_parts(dk):
        kk = k if dk == 0 else 1 - k
        for yy in range(2):

            def body(zz, carry):
                owner = (zz * 2 + yy) * 2 + kk
                at = pl.ds(pl.multiple_of(owner * cols, cols), cols)
                parts[dk, yy, zz] = scale * dot(low_t, x_ref[:, at], 1, 0)
                return carry

            lax.fori_loop(0, zs, body, 0)

    down_parts(1)
    send(parts.at[1], rc, dsem.at[0, 0], dsem.at[0, 1], sibling)
    down_parts(0)

    orders = [
        sorted(range(1, zs), key=lambda dz: (dz if zz + dz < zs else zs - dz, zz + dz >= zs))
        for zz in range(zs)
    ]

    def nth(i):
        if i == 0:
            return 0
        return sum(jnp.where(z == zz, orders[zz][i - 1], 0) for zz in range(zs))

    def w_from_z(i, c):
        dz = nth(i)
        piece = chunk(m, place(dz, 0, 0), c)
        arrived(piece, wsem_z.at[0, c, 0, dz], wsem_z.at[1, c, 0, dz], device(dz=1))
        from_above = z + dz < zs
        step = jnp.where(from_above, zs - 1, 1)
        at = jnp.where(from_above, lax.rem(dz + 1, zs), dz - 1)
        further = jnp.where(from_above, z, zs - 1 - z) > 0
        send(
            piece,
            piece,
            wsem_z.at[0, c, 1, dz],
            wsem_z.at[1, c, 0, at],
            (group, place(step, 0, 0)),
            further,
        )
        send(piece, piece, wsem_y.at[0, c, dz], wsem_y.at[1, c, dz], across_y)
        send(piece, piece, wsem_x.at[0, c, dz], wsem_x.at[1, c, dz], across_x)
        send(piece, piece, wsem_c.at[0, 0, c, dz], wsem_c.at[1, 0, c, dz], sibling)

    def w_from_y(i, c):
        dz = nth(i)
        slot = zs + dz
        piece = chunk(m, place(dz, 1, 0), c)
        arrived(piece, wsem_y.at[0, c, dz], wsem_y.at[1, c, dz], across_y)
        send(piece, piece, wsem_x.at[0, c, slot], wsem_x.at[1, c, slot], across_x)
        send(piece, piece, wsem_c.at[0, 0, c, slot], wsem_c.at[1, 0, c, slot], sibling)

    def w_from_x(i, dy, c):
        dz = nth(i)
        slot = dy * zs + dz
        piece = chunk(1 - m, place(dz, dy, 0), c)
        arrived(piece, wsem_x.at[0, c, slot], wsem_x.at[1, c, slot], across_x)
        send(piece, piece, wsem_c.at[0, 1, c, slot], wsem_c.at[1, 1, c, slot], sibling)

    def reduce_y(own, received, landing, ssem, rsem):
        own[0, 1 - y] = own[0, 1 - y] + received[1 - y]
        send(own.at[0, 1 - y], landing, ssem, rsem, across_y)
        own[0, y] = own[0, y] + received[y]

    def reduce_z(own, received, landing, sem):
        own[0, y] = own[0, y] + received[...]
        for dz in range(1, zs):
            send(
                own.at[0, y, lax.rem(z + zs - dz, zs)],
                landing.at[dz],
                sem.at[0, dz],
                sem.at[1, dz],
                device(dz=-dz),
            )

    def reduce_end(own, landing, sem):
        total = own[0, y, z]
        for dz in range(1, zs):
            arrived(landing.at[dz], sem.at[0, dz], sem.at[1, dz], device(dz=dz))
            total = total + landing[dz]
        return total

    def w_round(i):
        for c in range(2):
            w_from_y(i, c)
            if i + 1 < zs:
                w_from_z(i + 1, c)

    gather_middle(abuf, asem)
    arrived(rc, dsem.at[0, 0], dsem.at[0, 1], sibling)
    reduce_y(parts, rc, ry, dsem.at[1, 0], dsem.at[1, 1])
    w_round(0)
    w_round(1)
    arrived(ry, dsem.at[1, 0], dsem.at[1, 1], across_y)
    reduce_z(parts, ry, rz, dzsem)
    gather_end(abuf, asem)

    hidden = jnp.zeros((x_ref.shape[0], 2 * rank), F32)

    def hidden_step(owner, total):
        at = pl.ds(pl.multiple_of(owner * cols, cols), cols)
        return total + dot(x_ref[:, at], abuf[owner], 1, 0)

    hidden = lax.fori_loop(0, n, hidden_step, hidden).astype(BF16)
    rows = 2 * rank // n
    hidden_t = hidden.astype(F32).T.astype(BF16)
    ups = scale * jnp.concatenate(
        [
            dot(hidden_t[p * rank : (p + 1) * rank], g_ref[:, p * width : (p + 1) * width], 1, 0)
            for p in range(2)
        ],
        axis=0,
    )
    for owner in range(n):
        kk, yy, zz = owner % 2, owner // 2 % 2, owner // 4
        dk = lax.rem(k + kk, 2)
        uparts[dk, yy, zz] = ups[owner * rows : (owner + 1) * rows]
    send(uparts.at[1], uc, usem.at[0, 0], usem.at[0, 1], sibling)

    for i in range(2, zs):
        w_round(i)
        if i == 2:
            arrived(uc, usem.at[0, 0], usem.at[0, 1], sibling)
            reduce_y(uparts, uc, uy, usem.at[1, 0], usem.at[1, 1])
    arrived(uy, usem.at[1, 0], usem.at[1, 1], across_y)
    reduce_z(uparts, uy, uz, uzsem)
    down_ref[...] = reduce_end(parts, rz, dzsem)
    ubuf[me] = reduce_end(uparts, uz, uzsem)
    gather_start(ubuf, gsem)
    for i in range(zs):
        for c in range(2):
            w_from_x(i, 1, c)
            if i + 1 < zs:
                w_from_x(i + 1, 0, c)
        if i == 1:
            gather_middle(ubuf, gsem)
    gather_end(ubuf, gsem)
    for p in range(2):
        at = m if p == 0 else 1 - m
        for c in range(2):
            for dz in range(zs):
                for dy in range(2):
                    slot = dy * zs + dz
                    arrived(
                        chunk(at, place(dz, dy, 1), c),
                        wsem_c.at[0, p, c, slot],
                        wsem_c.at[1, p, c, slot],
                        sibling,
                    )
    for copy, when in sends:
        if when is None:
            copy.wait_send()
        else:
            pl.when(when)(copy.wait_send)
    keep_first.wait()
    keep_second.wait()


def rows_kernel(row_blocks, table_ref, w_ref, a_ref, g_ref, low_ref, out_ref, dense):
    shard = pl.program_id(1) * pl.num_programs(0) + pl.program_id(0)
    full = w_ref.shape[3]
    block = w_ref.shape[-1]
    per_shard = out_ref.shape[1] // block
    col_blocks = g_ref.shape[1] // (2 * block)
    zero = jnp.zeros((block, block), BF16)
    for m in range(2):
        for r in range(per_shard):
            for c in range(col_blocks):
                code = table_ref[(m * row_blocks + shard * per_shard + r) * col_blocks + c]
                at = jnp.maximum(code, 0)
                taken = w_ref[m, at // full, 0, lax.rem(at, full)]
                col = (m * col_blocks + c) * block
                dense[r * block : (r + 1) * block, col : col + block] = jnp.where(
                    code >= 0, taken, zero
                )
    total = dot(g_ref[...], dense[...], 1, 1)
    total = total + adapter_scale * dot(low_ref[...], a_ref[...], 1, 1)
    out_ref[...] = total.astype(BF16)


def on_device(
    inputs, key_value_gradient, kept_frozen_blocks, kept, adapter_down_matrices, adapter_up_matrices
):
    n = lax.axis_size("fsdp")
    zs = n // 4
    tokens, model_width = inputs.shape
    slot_count = kept_frozen_blocks.shape[1]
    block = kept_frozen_blocks.shape[-1]
    row_blocks, col_blocks = kept.shape[1:]
    per_shard = row_blocks // n
    full = 4 * per_shard
    rank, width = adapter_up_matrices.shape[1:]
    cols = adapter_down_matrices.shape[0]
    rows = 2 * rank // n
    scale = adapter_scale / math.sqrt(tokens * n)

    flat = kept.reshape(2, n, per_shard * col_blocks)
    before = jnp.cumsum(flat, axis=-1) - flat
    counts = flat.sum(axis=-1)
    half = (jnp.arange(n, dtype=jnp.int32) // (n // 2))[None, :, None]
    code = jnp.where(
        before < full,
        half * full + before,
        (1 - half) * full + (2 * full - counts[:, :, None]) + before - full,
    )
    table = jnp.where(flat > 0, code, -1).reshape(-1).astype(jnp.int32)
    own_counts = lax.dynamic_index_in_dim(counts, lax.axis_index("fsdp"), 1, keepdims=False)

    vmem = pl.BlockSpec(memory_space=pltpu.VMEM)
    smem = pl.BlockSpec(memory_space=pltpu.SMEM)
    hbm = pl.BlockSpec(memory_space=pl.ANY)
    dma = pltpu.SemaphoreType.DMA
    wbuf, abuf, low, down_t, ubuf = pl.pallas_call(
        functools.partial(exchange_kernel, n, scale),
        out_shape=(
            jax.ShapeDtypeStruct((2, n, full, block, block), BF16),
            jax.ShapeDtypeStruct((n, cols, 2 * rank), BF16),
            jax.ShapeDtypeStruct((tokens, 2 * rank), BF16),
            jax.ShapeDtypeStruct((2 * rank, cols), F32),
            jax.ShapeDtypeStruct((n, rows, width), F32),
        ),
        in_specs=[smem, vmem, vmem, vmem, vmem, vmem],
        out_specs=(hbm, vmem, vmem, vmem, vmem),
        scratch_shapes=[
            pltpu.VMEM((2, full // 2, block, block), BF16),
            pltpu.VMEM((2, per_shard, block, block), BF16),
            pltpu.VMEM((2, 2, zs, 2 * rank, cols), F32),
            pltpu.VMEM((2, zs, 2 * rank, cols), F32),
            pltpu.VMEM((zs, 2 * rank, cols), F32),
            pltpu.VMEM((zs, 2 * rank, cols), F32),
            pltpu.VMEM((2, 2, zs, rows, width), F32),
            pltpu.VMEM((2, zs, rows, width), F32),
            pltpu.VMEM((zs, rows, width), F32),
            pltpu.VMEM((zs, rows, width), F32),
            dma((3, 2, 2 * zs)),
            dma((2, 2, 2, zs)),
            dma((2, 2, zs)),
            dma((2, 2, 2 * zs)),
            dma((2, 2, 2, 2 * zs)),
            dma((2,)),
            dma((2, 2)),
            dma((2, zs)),
            dma((2, 2)),
            dma((2, zs)),
            dma((3, 2, 2 * zs)),
            dma((2,)),
        ],
        compiler_params=pltpu.CompilerParams(
            collective_id=0, has_side_effects=True, vmem_limit_bytes=48 * 2**20
        ),
        name="exchange",
    )(
        own_counts,
        inputs,
        key_value_gradient,
        kept_frozen_blocks,
        adapter_down_matrices,
        adapter_up_matrices,
    )

    shard_cols = per_shard * block
    grad_inputs = pl.pallas_call(
        functools.partial(rows_kernel, row_blocks),
        out_shape=jax.ShapeDtypeStruct((tokens, model_width), BF16),
        grid_spec=pltpu.PrefetchScalarGridSpec(
            num_scalar_prefetch=1,
            grid=(n // 2, 2),
            in_specs=[
                pl.BlockSpec(
                    (2, 2, 1, full, block, block), lambda p, h, t: (0, 0, p, 0, 0, 0)
                ),
                pl.BlockSpec((shard_cols, 2 * rank), lambda p, h, t: (h * (n // 2) + p, 0)),
                pl.BlockSpec((tokens, 2 * width), lambda p, h, t: (0, 0)),
                pl.BlockSpec((tokens, 2 * rank), lambda p, h, t: (0, 0)),
            ],
            out_specs=pl.BlockSpec((tokens, shard_cols), lambda p, h, t: (0, h * (n // 2) + p)),
            scratch_shapes=[pltpu.VMEM((shard_cols, 2 * width), BF16)],
        ),
        compiler_params=pltpu.CompilerParams(vmem_limit_bytes=40 * 2**20),
        name="rows",
    )(
        table,
        wbuf.reshape(2, 2, n // 2, full, block, block),
        abuf.reshape(n * cols, 2 * rank),
        key_value_gradient,
        low,
    )
    return grad_inputs, down_t.T, ubuf.reshape(2, rank, width)


def solution(mesh):
    return jax.shard_map(
        on_device,
        mesh=mesh,
        in_specs=(
            P(("groups", "fsdp"), None),
            P(("groups", "fsdp"), None),
            P(None, "fsdp", None, None),
            P(),
            P(("groups", "fsdp"), None),
            P("groups", None, None),
        ),
        out_specs=(
            P(("groups", "fsdp"), None),
            P(("groups", "fsdp"), None),
            P("groups", None, None),
        ),
        check_vma=False,
    )
```

```python
import functools
import math

import jax
import jax.numpy as jnp
from jax import lax
from jax.experimental import pallas as pl
from jax.experimental.pallas import tpu as pltpu
from jax.sharding import PartitionSpec as P

adapter_scale = 0.5
F32 = jnp.float32
BF16 = jnp.bfloat16


def dot(a, b, ca, cb):
    return lax.dot_general(a, b, (((ca,), (cb,)), ((), ())), preferred_element_type=F32)


def exchange_kernel(
    n,
    scale,
    count_ref,
    x_hbm,
    g_ref,
    kfb_ref,
    a_ref,
    b_ref,
    wbuf,
    abuf,
    low_ref,
    down_ref,
    ubuf,
    x_ref,
    wown,
    ovf,
    parts,
    rc,
    ry,
    rz,
    uparts,
    uc,
    uy,
    uz,
    asem,
    wsem_z,
    wsem_y,
    wsem_x,
    wsem_c,
    osem,
    dsem,
    dzsem,
    usem,
    uzsem,
    gsem,
    lsem,
    xsem,
):
    load = pltpu.make_async_copy(x_hbm, x_ref, xsem)
    load.start()
    zs = n // 4
    group = lax.axis_index("groups")
    me = lax.axis_index("fsdp")
    k = lax.rem(me, 2)
    y = lax.rem(me // 2, 2)
    z = me // 4
    m = lax.rem(group, 2)
    other_group = group + 1 - 2 * m

    def place(dz, dy, dk):
        zz = lax.rem(z + dz, zs)
        yy = y if dy == 0 else 1 - y
        kk = k if dk == 0 else 1 - k
        return (zz * 2 + yy) * 2 + kk

    def device(dz=0, dy=0, dk=0, dx=0):
        return (group if dx == 0 else other_group, place(dz % zs, dy, dk))

    sends = []

    def send(src, dst, ssem, rsem, target, when=None):
        copy = pltpu.make_async_remote_copy(
            src_ref=src,
            dst_ref=dst,
            send_sem=ssem,
            recv_sem=rsem,
            device_id=target,
            device_id_type=pl.DeviceIdType.MESH,
        )
        if when is None:
            copy.start()
        else:
            pl.when(when)(copy.start)
        sends.append((copy, when))

    def arrived(ref, ssem, rsem, source):
        pltpu.make_async_remote_copy(
            src_ref=ref,
            dst_ref=ref,
            send_sem=ssem,
            recv_sem=rsem,
            device_id=source,
            device_id_type=pl.DeviceIdType.MESH,
        ).wait_recv()

    sibling = device(dk=1)
    across_y = device(dy=1)
    across_x = device(dx=1)
    partners = [sibling, across_y, across_x] + [device(dz=dz) for dz in range(1, zs)]
    barrier = pltpu.get_barrier_semaphore()
    for partner in partners:
        pl.semaphore_signal(
            barrier, inc=1, device_id=partner, device_id_type=pl.DeviceIdType.MESH
        )
    pl.semaphore_wait(barrier, len(partners))

    def gather_start(buf, sem):
        own = buf.at[me]
        for dz in range(1, zs):
            send(own, own, sem.at[0, 0, dz], sem.at[0, 1, dz], device(dz=-dz))
        send(own, own, sem.at[1, 0, 0], sem.at[1, 1, 0], across_y)
        send(own, own, sem.at[2, 0, 0], sem.at[2, 1, 0], sibling)

    def gather_middle(buf, sem):
        for dz in range(1, zs):
            piece = buf.at[place(dz, 0, 0)]
            arrived(piece, sem.at[0, 0, dz], sem.at[0, 1, dz], device(dz=dz))
            send(piece, piece, sem.at[1, 0, dz], sem.at[1, 1, dz], across_y)
            send(piece, piece, sem.at[2, 0, dz], sem.at[2, 1, dz], sibling)
        for dz in range(zs):
            piece = buf.at[place(dz, 1, 0)]
            arrived(piece, sem.at[1, 0, dz], sem.at[1, 1, dz], across_y)
            send(piece, piece, sem.at[2, 0, zs + dz], sem.at[2, 1, zs + dz], sibling)

    def gather_end(buf, sem):
        for dz in range(zs):
            for dy in range(2):
                slot = dy * zs + dz
                arrived(
                    buf.at[place(dz, dy, 1)], sem.at[2, 0, slot], sem.at[2, 1, slot], sibling
                )

    slots = kfb_ref.shape[1]
    per_shard = slots // 5
    full = 4 * per_shard
    least = 3 * per_shard

    send(kfb_ref.at[:, pl.ds(full, per_shard)], ovf, osem.at[0], osem.at[1], device(dz=zs // 2))
    abuf[me] = a_ref[...]
    gather_start(abuf, asem)

    half = full // 2

    def chunk(p, owner, c):
        return wbuf.at[p, owner, pl.ds(c * half, half)]

    def w_start(own, c):
        mine = own.at[m, pl.ds(0, half)]
        to = chunk(m, me, c)
        send(
            mine,
            to,
            wsem_z.at[0, c, 0, 1],
            wsem_z.at[1, c, 0, 1],
            device(dz=-1),
            z > 0,
        )
        send(
            mine,
            to,
            wsem_z.at[0, c, 0, zs - 1],
            wsem_z.at[1, c, 0, zs - 1],
            device(dz=1),
            z < zs - 1,
        )
        send(mine, to, wsem_y.at[0, c, 0], wsem_y.at[1, c, 0], across_y)
        for p in range(2):
            at = m if p == 0 else 1 - m
            send(
                own.at[at, pl.ds(0, half)],
                chunk(at, me, c),
                wsem_c.at[0, p, c, 0],
                wsem_c.at[1, p, c, 0],
                sibling,
            )

    w_start(kfb_ref, 0)
    keep_first = pltpu.make_async_copy(
        kfb_ref.at[:, pl.ds(0, half)], wbuf.at[:, me, pl.ds(0, half)], lsem.at[0]
    )
    keep_first.start()

    wown[:, 0 : least - half] = kfb_ref[:, half:least]
    rank = b_ref.shape[1]
    width = b_ref.shape[2]
    lows = [dot(g_ref[:, p * width : (p + 1) * width], b_ref[p], 1, 1) for p in range(2)]
    low_ref[...] = jnp.concatenate(lows, axis=1).astype(BF16)

    arrived(ovf, osem.at[0], osem.at[1], device(dz=zs // 2))
    for p in range(2):
        held = count_ref[p]
        for t in range(per_shard):
            slot = least + t
            extra = ovf[p, jnp.clip(slot - held, 0, per_shard - 1)]
            wown[p, slot - half] = jnp.where(slot < held, kfb_ref[p, slot], extra)

    w_start(wown, 1)
    keep_second = pltpu.make_async_copy(
        wown, wbuf.at[:, me, pl.ds(half, half)], lsem.at[1]
    )
    keep_second.start()

    low_t = low_ref[...].astype(F32).T.astype(BF16)
    cols = a_ref.shape[0]

    def down_parts(dk):
        kk = k if dk == 0 else 1 - k
        for yy in range(2):

            def body(zz, carry):
                owner = (zz * 2 + yy) * 2 + kk
                at = pl.ds(pl.multiple_of(owner * cols, cols), cols)
                parts[dk, yy, zz] = scale * dot(low_t, x_ref[:, at], 1, 0)
                return carry

            lax.fori_loop(0, zs, body, 0)

    load.wait()
    down_parts(1)
    send(parts.at[1], rc, dsem.at[0, 0], dsem.at[0, 1], sibling)
    down_parts(0)

    orders = [
        sorted(range(1, zs), key=lambda dz: (dz if zz + dz < zs else zs - dz, zz + dz >= zs))
        for zz in range(zs)
    ]

    def nth(i):
        if i == 0:
            return 0
        return sum(jnp.where(z == zz, orders[zz][i - 1], 0) for zz in range(zs))

    def w_from_z(i, c):
        dz = nth(i)
        piece = chunk(m, place(dz, 0, 0), c)
        arrived(piece, wsem_z.at[0, c, 0, dz], wsem_z.at[1, c, 0, dz], device(dz=1))
        from_above = z + dz < zs
        step = jnp.where(from_above, zs - 1, 1)
        at = jnp.where(from_above, lax.rem(dz + 1, zs), dz - 1)
        further = jnp.where(from_above, z, zs - 1 - z) > 0
        send(
            piece,
            piece,
            wsem_z.at[0, c, 1, dz],
            wsem_z.at[1, c, 0, at],
            (group, place(step, 0, 0)),
            further,
        )
        send(piece, piece, wsem_y.at[0, c, dz], wsem_y.at[1, c, dz], across_y)
        send(piece, piece, wsem_x.at[0, c, dz], wsem_x.at[1, c, dz], across_x)
        send(piece, piece, wsem_c.at[0, 0, c, dz], wsem_c.at[1, 0, c, dz], sibling)

    def w_from_y(i, c):
        dz = nth(i)
        slot = zs + dz
        piece = chunk(m, place(dz, 1, 0), c)
        arrived(piece, wsem_y.at[0, c, dz], wsem_y.at[1, c, dz], across_y)
        send(piece, piece, wsem_x.at[0, c, slot], wsem_x.at[1, c, slot], across_x)
        send(piece, piece, wsem_c.at[0, 0, c, slot], wsem_c.at[1, 0, c, slot], sibling)

    def w_from_x(i, dy, c):
        dz = nth(i)
        slot = dy * zs + dz
        piece = chunk(1 - m, place(dz, dy, 0), c)
        arrived(piece, wsem_x.at[0, c, slot], wsem_x.at[1, c, slot], across_x)
        send(piece, piece, wsem_c.at[0, 1, c, slot], wsem_c.at[1, 1, c, slot], sibling)

    def reduce_y(own, received, landing, ssem, rsem):
        own[0, 1 - y] = own[0, 1 - y] + received[1 - y]
        send(own.at[0, 1 - y], landing, ssem, rsem, across_y)
        own[0, y] = own[0, y] + received[y]

    def reduce_z(own, received, landing, sem):
        own[0, y] = own[0, y] + received[...]
        for dz in range(1, zs):
            send(
                own.at[0, y, lax.rem(z + zs - dz, zs)],
                landing.at[dz],
                sem.at[0, dz],
                sem.at[1, dz],
                device(dz=-dz),
            )

    def reduce_end(own, landing, sem):
        total = own[0, y, z]
        for dz in range(1, zs):
            arrived(landing.at[dz], sem.at[0, dz], sem.at[1, dz], device(dz=dz))
            total = total + landing[dz]
        return total

    def w_round(i):
        for c in range(2):
            w_from_y(i, c)
            if i + 1 < zs:
                w_from_z(i + 1, c)

    gather_middle(abuf, asem)
    arrived(rc, dsem.at[0, 0], dsem.at[0, 1], sibling)
    reduce_y(parts, rc, ry, dsem.at[1, 0], dsem.at[1, 1])
    w_round(0)
    w_round(1)
    arrived(ry, dsem.at[1, 0], dsem.at[1, 1], across_y)
    reduce_z(parts, ry, rz, dzsem)
    gather_end(abuf, asem)

    hidden = jnp.zeros((x_ref.shape[0], 2 * rank), F32)

    def hidden_step(owner, total):
        at = pl.ds(pl.multiple_of(owner * cols, cols), cols)
        return total + dot(x_ref[:, at], abuf[owner], 1, 0)

    hidden = lax.fori_loop(0, n, hidden_step, hidden).astype(BF16)
    rows = 2 * rank // n
    hidden_t = hidden.astype(F32).T.astype(BF16)
    ups = scale * jnp.concatenate(
        [
            dot(hidden_t[p * rank : (p + 1) * rank], g_ref[:, p * width : (p + 1) * width], 1, 0)
            for p in range(2)
        ],
        axis=0,
    )
    for owner in range(n):
        kk, yy, zz = owner % 2, owner // 2 % 2, owner // 4
        dk = lax.rem(k + kk, 2)
        uparts[dk, yy, zz] = ups[owner * rows : (owner + 1) * rows]
    send(uparts.at[1], uc, usem.at[0, 0], usem.at[0, 1], sibling)

    for i in range(2, zs):
        w_round(i)
        if i == 2:
            arrived(uc, usem.at[0, 0], usem.at[0, 1], sibling)
            reduce_y(uparts, uc, uy, usem.at[1, 0], usem.at[1, 1])
    arrived(uy, usem.at[1, 0], usem.at[1, 1], across_y)
    reduce_z(uparts, uy, uz, uzsem)
    down_ref[...] = reduce_end(parts, rz, dzsem)
    ubuf[me] = reduce_end(uparts, uz, uzsem)
    gather_start(ubuf, gsem)
    for i in range(zs):
        for c in range(2):
            w_from_x(i, 1, c)
            if i + 1 < zs:
                w_from_x(i + 1, 0, c)
        if i == 1:
            gather_middle(ubuf, gsem)
    gather_end(ubuf, gsem)
    for p in range(2):
        at = m if p == 0 else 1 - m
        for c in range(2):
            for dz in range(zs):
                for dy in range(2):
                    slot = dy * zs + dz
                    arrived(
                        chunk(at, place(dz, dy, 1), c),
                        wsem_c.at[0, p, c, slot],
                        wsem_c.at[1, p, c, slot],
                        sibling,
                    )
    for copy, when in sends:
        if when is None:
            copy.wait_send()
        else:
            pl.when(when)(copy.wait_send)
    keep_first.wait()
    keep_second.wait()


def rows_kernel(row_blocks, table_ref, w_ref, a_ref, g_ref, low_ref, out_ref):
    shard = pl.program_id(1) * pl.num_programs(0) + pl.program_id(0)
    full = w_ref.shape[3]
    block = w_ref.shape[-1]
    per_shard = out_ref.shape[1] // block
    col_blocks = g_ref.shape[1] // (2 * block)
    zero = jnp.zeros((block, block), BF16)

    def taken(m, r, c):
        code = table_ref[(m * row_blocks + shard * per_shard + r) * col_blocks + c]
        at = jnp.maximum(code, 0)
        return jnp.where(code >= 0, w_ref[m, at // full, 0, lax.rem(at, full)], zero)

    rows = [
        jnp.concatenate([taken(m, r, c) for m in range(2) for c in range(col_blocks)], axis=1)
        for r in range(per_shard)
    ]
    total = dot(g_ref[...], jnp.concatenate(rows, axis=0), 1, 1)
    total = total + adapter_scale * dot(low_ref[...], a_ref[...], 1, 1)
    out_ref[...] = total.astype(BF16)


def on_device(
    inputs, key_value_gradient, kept_frozen_blocks, kept, adapter_down_matrices, adapter_up_matrices
):
    n = lax.axis_size("fsdp")
    zs = n // 4
    tokens, model_width = inputs.shape
    slot_count = kept_frozen_blocks.shape[1]
    block = kept_frozen_blocks.shape[-1]
    row_blocks, col_blocks = kept.shape[1:]
    per_shard = row_blocks // n
    full = 4 * per_shard
    rank, width = adapter_up_matrices.shape[1:]
    cols = adapter_down_matrices.shape[0]
    rows = 2 * rank // n
    scale = adapter_scale / math.sqrt(tokens * n)

    flat = kept.reshape(2, n, per_shard * col_blocks)
    before = jnp.cumsum(flat, axis=-1) - flat
    counts = flat.sum(axis=-1)
    half = (jnp.arange(n, dtype=jnp.int32) // (n // 2))[None, :, None]
    code = jnp.where(
        before < full,
        half * full + before,
        (1 - half) * full + (2 * full - counts[:, :, None]) + before - full,
    )
    table = jnp.where(flat > 0, code, -1).reshape(-1).astype(jnp.int32)
    own_counts = lax.dynamic_index_in_dim(counts, lax.axis_index("fsdp"), 1, keepdims=False)

    vmem = pl.BlockSpec(memory_space=pltpu.VMEM)
    smem = pl.BlockSpec(memory_space=pltpu.SMEM)
    hbm = pl.BlockSpec(memory_space=pl.ANY)
    dma = pltpu.SemaphoreType.DMA
    wbuf, abuf, low, down_t, ubuf = pl.pallas_call(
        functools.partial(exchange_kernel, n, scale),
        out_shape=(
            jax.ShapeDtypeStruct((2, n, full, block, block), BF16),
            jax.ShapeDtypeStruct((n, cols, 2 * rank), BF16),
            jax.ShapeDtypeStruct((tokens, 2 * rank), BF16),
            jax.ShapeDtypeStruct((2 * rank, cols), F32),
            jax.ShapeDtypeStruct((n, rows, width), F32),
        ),
        in_specs=[smem, hbm, vmem, vmem, vmem, vmem],
        out_specs=(hbm, vmem, vmem, vmem, vmem),
        scratch_shapes=[
            pltpu.VMEM((tokens, model_width), BF16),
            pltpu.VMEM((2, full // 2, block, block), BF16),
            pltpu.VMEM((2, per_shard, block, block), BF16),
            pltpu.VMEM((2, 2, zs, 2 * rank, cols), F32),
            pltpu.VMEM((2, zs, 2 * rank, cols), F32),
            pltpu.VMEM((zs, 2 * rank, cols), F32),
            pltpu.VMEM((zs, 2 * rank, cols), F32),
            pltpu.VMEM((2, 2, zs, rows, width), F32),
            pltpu.VMEM((2, zs, rows, width), F32),
            pltpu.VMEM((zs, rows, width), F32),
            pltpu.VMEM((zs, rows, width), F32),
            dma((3, 2, 2 * zs)),
            dma((2, 2, 2, zs)),
            dma((2, 2, zs)),
            dma((2, 2, 2 * zs)),
            dma((2, 2, 2, 2 * zs)),
            dma((2,)),
            dma((2, 2)),
            dma((2, zs)),
            dma((2, 2)),
            dma((2, zs)),
            dma((3, 2, 2 * zs)),
            dma((2,)),
            dma(()),
        ],
        compiler_params=pltpu.CompilerParams(
            collective_id=0, has_side_effects=True, vmem_limit_bytes=56 * 2**20
        ),
        name="exchange",
    )(
        own_counts,
        inputs,
        key_value_gradient,
        kept_frozen_blocks,
        adapter_down_matrices,
        adapter_up_matrices,
    )

    shard_cols = per_shard * block
    grad_inputs = pl.pallas_call(
        functools.partial(rows_kernel, row_blocks),
        out_shape=jax.ShapeDtypeStruct((tokens, model_width), BF16),
        grid_spec=pltpu.PrefetchScalarGridSpec(
            num_scalar_prefetch=1,
            grid=(n // 2, 2),
            in_specs=[
                pl.BlockSpec(
                    (2, 2, 1, full, block, block), lambda p, h, t: (0, 0, p, 0, 0, 0)
                ),
                pl.BlockSpec((shard_cols, 2 * rank), lambda p, h, t: (h * (n // 2) + p, 0)),
                pl.BlockSpec((tokens, 2 * width), lambda p, h, t: (0, 0)),
                pl.BlockSpec((tokens, 2 * rank), lambda p, h, t: (0, 0)),
            ],
            out_specs=pl.BlockSpec((tokens, shard_cols), lambda p, h, t: (0, h * (n // 2) + p)),
        ),
        compiler_params=pltpu.CompilerParams(vmem_limit_bytes=40 * 2**20),
        name="rows",
    )(
        table,
        wbuf.reshape(2, 2, n // 2, full, block, block),
        abuf.reshape(n * cols, 2 * rank),
        key_value_gradient,
        low,
    )
    return grad_inputs, down_t.T, ubuf.reshape(2, rank, width)


def solution(mesh):
    return jax.shard_map(
        on_device,
        mesh=mesh,
        in_specs=(
            P(("groups", "fsdp"), None),
            P(("groups", "fsdp"), None),
            P(None, "fsdp", None, None),
            P(),
            P(("groups", "fsdp"), None),
            P("groups", None, None),
        ),
        out_specs=(
            P(("groups", "fsdp"), None),
            P(("groups", "fsdp"), None),
            P("groups", None, None),
        ),
        check_vma=False,
    )
```
